32 devices in a mesh: depth: 4 (over y, x), plane: 8 (over z, core).
Axes of the slice: x: 2, y: 2, z: 4, core: 2. Of those that a mesh axis runs over, the one named last changes fastest.
Arguments:
- volume: bfloat16 [16, 32, 128], P('depth', 'plane'), may hold values from -6 to 6
- cotangent: float32 [16, 32, 128], P('depth', 'plane'), may hold values from -6 to 6
- kernel_in: bfloat16 [27, 32], replicated, may hold values from -1.25 to 1.25
- kernel_mid: bfloat16 [27, 32, 32], replicated, may hold values from -0.21875 to 0.21875
- kernel_out: bfloat16 [27, 32], replicated, may hold values from -0.21875 to 0.21875
- measured: float32 [16, 32, 1024], P('depth'), may hold values from -24 to 24
- angle_ids: int32 [8], replicated, may hold values from 0 to 31, as said below
- ray_bins: int32 [8, 32, 128], P(None, 'plane'), may hold values from 0 to 1023, as said below
Outputs:
- grad_volume: float32 [16, 32, 128], P('depth', 'plane')
- grad_kernel_in: float32 [27, 32], replicated
- grad_kernel_mid: float32 [27, 32, 32], replicated
- grad_kernel_out: float32 [27, 32], replicated
The draws below stay inside these ranges and needn't reach their ends.
Inputs may be any that keep to these rules, and one draw needn't show every extreme that they name: `angle_ids`: each entry names a measured view; the entries are distinct. `ray_bins`: for each view a, the bins follow parallel-beam geometry: a cell's bin is the detector position of its centre projected along the direction of view angle_ids[a], clipped at the detector's ends.
All inputs are finite; a program needn't handle non-finite values.
Results may differ from the reference program's by a relative error of at most 0.0051.
Values may be sent and summed in bfloat16 or wider, within the bound.
A program may use at most 64 MiB of HBM per device.

```python
import jax
import jax.numpy as jnp
from jax import lax

C = 32
BINS = 1024
ANG = 8
ANG_ALL = 32
W = 128
NZ = 16
NH = 32


def view_table(key):
    order = jax.random.permutation(jax.random.fold_in(key, 11), ANG_ALL)
    return order[:ANG].astype(jnp.int32)


def draw_angle_ids(key, part):
    return view_table(key)


def draw_ray_bins(key, part):
    views = view_table(key)
    tangent = 2 * views - ANG_ALL
    cosine_num = ANG_ALL * ANG_ALL - tangent * tangent
    sine_num = 2 * tangent * ANG_ALL
    denom = ANG_ALL * ANG_ALL + tangent * tangent
    rows_twice = 2 * jnp.arange(NH, dtype=jnp.int32) - (NH - 1)
    cells_twice = 2 * jnp.arange(W, dtype=jnp.int32) - (W - 1)
    stretch = BINS // min(W, NH) + 1
    along = cells_twice[None, None, :] * cosine_num[:, None, None] + rows_twice[None, :, None] * sine_num[:, None, None]
    placed = BINS // 2 + along * stretch // (2 * denom[:, None, None])
    return jnp.clip(placed, 0, BINS - 1).astype(jnp.int32)


def block_levels(own_key, dims, cuts, low, largest):
    level = 1.0
    for axis_at, shards_of in cuts:
        heights = jax.random.uniform(jax.random.fold_in(jax.random.fold_in(own_key, 6), axis_at), (shards_of,), jnp.float32, low / len(cuts), largest / len(cuts))
        level = level * jnp.repeat(jnp.exp(heights), dims[axis_at] // shards_of).reshape((-1,) + (1,) * (len(dims) - 1 - axis_at))
    return level


def normal_values(stream_key, shape, spread, most, cuts=(), kind=jnp.bfloat16):
    factor_of = block_levels(stream_key, shape, cuts, -0.22, 0.18) if cuts else 1.0
    values = jax.random.normal(stream_key, shape, jnp.float32) * spread * factor_of
    return jnp.minimum(jnp.maximum(values, -most), most).astype(kind)


def setup_inputs(seed: int = 0) -> dict:
    keys = jax.random.split(jax.random.key(seed), 9)
    return {
        "volume": normal_values(keys[0], (NZ, NH, W), 1.0, 6.0, ((0, 4), (1, 8))),
        "cotangent": normal_values(keys[1], (NZ, NH, W), 1.0, 6.0, ((0, 4), (1, 8)), jnp.float32),
        "kernel_in": normal_values(keys[2], (27, C), 27 ** -0.5, 1.25),
        "kernel_mid": normal_values(keys[3], (27, C, C), (27 * C) ** -0.5, 0.21875),
        "kernel_out": normal_values(keys[4], (27, C), (27 * C) ** -0.5, 0.21875),
        "measured": normal_values(keys[5], (NZ, ANG_ALL, BINS), 4.0, 24.0, ((0, 4),), jnp.float32),
        "angle_ids": draw_angle_ids(jax.random.fold_in(keys[8], 71), 0),
        "ray_bins": draw_ray_bins(jax.random.fold_in(keys[8], 71), 0),
    }


delta_scale = 6.0

def shifts():
    return [(step_z, step_y, step_x) for step_z in (-1, 0, 1) for step_y in (-1, 0, 1) for step_x in (-1, 0, 1)]

def pad_cells(field):
    return jnp.pad(field, ((0, 0), (1, 1), (1, 1), (1, 1)))

def window_at(padded, start_z, start_y, start_x, extent):
    return lax.slice(padded, (0, start_z, start_y, start_x), (padded.shape[0], start_z + extent[0], start_y + extent[1], start_x + extent[2]))

def forward_conv(padded, kernel, extent):
    summed = jnp.zeros((kernel.shape[1],) + tuple(extent), jnp.float32)
    for position, (step_z, step_y, step_x) in enumerate(shifts()):
        window = window_at(padded, 1 + step_z, 1 + step_y, 1 + step_x, extent)
        summed = summed + jnp.einsum('oc,czhw->ozhw', kernel[position].astype(jnp.float32), window.astype(jnp.float32))
    return summed

def adjoint_conv(padded, kernel, extent):
    summed = jnp.zeros((kernel.shape[2],) + tuple(extent), jnp.float32)
    for position, (step_z, step_y, step_x) in enumerate(shifts()):
        window = window_at(padded, 1 - step_z, 1 - step_y, 1 - step_x, extent)
        summed = summed + jnp.einsum('oc,ozhw->czhw', kernel[position].astype(jnp.float32), window.astype(jnp.float32))
    return summed

def kernel_grad(grad_out, padded_in, extent):
    pieces = []
    for position, (step_z, step_y, step_x) in enumerate(shifts()):
        window = window_at(padded_in, 1 + step_z, 1 + step_y, 1 + step_x, extent)
        pieces.append(jnp.einsum('ozhw,czhw->oc', grad_out.astype(jnp.float32), window.astype(jnp.float32)))
    return jnp.stack(pieces)

def silu_slope(value):
    sigma = jax.nn.sigmoid(value)
    return sigma * (1.0 + value * (1.0 - sigma))

def project_pair(first, second, ray_bins):
    slices = first.shape[0]
    flattened = jnp.concatenate((first.reshape(slices, -1), second.reshape(slices, -1)), axis=0).T

    def one_view(bins_view):
        return jax.ops.segment_sum(flattened, bins_view.reshape(-1), num_segments=BINS)
    per_view = lax.map(one_view, ray_bins)
    stacked = jnp.transpose(per_view, (2, 0, 1))
    return (stacked[:slices], stacked[slices:])

def back_project(rays, ray_bins):

    def accumulate(summed, view_pair):
        rays_view, bins_view = view_pair
        return (summed + jnp.take(rays_view, bins_view.reshape(-1), axis=1), None)
    initial = jnp.zeros((rays.shape[0], ray_bins.shape[1] * ray_bins.shape[2]), rays.dtype)
    summed = lax.scan(accumulate, initial, (jnp.transpose(rays, (1, 0, 2)), ray_bins))[0]
    return summed.reshape(rays.shape[0], ray_bins.shape[1], ray_bins.shape[2])

def curvature(residual):
    ratio = residual / delta_scale
    inner = 1.0 + ratio * ratio
    return 1.0 / (inner * jnp.sqrt(inner))

def reference(volume, cotangent, kernel_in, kernel_mid, kernel_out, measured, angle_ids, ray_bins):
    extent = volume.shape
    first_in = kernel_in[:, :, None]
    last_out = kernel_out[:, None, :]
    source_pad = pad_cells(volume[None])
    pre_first = forward_conv(source_pad, first_in, extent)
    act_first = jax.nn.silu(pre_first).astype(jnp.bfloat16)
    slope_first = silu_slope(pre_first)
    first_pad = pad_cells(act_first)
    pre_second = forward_conv(first_pad, kernel_mid, extent)
    act_second = jax.nn.silu(pre_second).astype(jnp.bfloat16)
    slope_second = silu_slope(pre_second)
    second_pad = pad_cells(act_second)
    residue = forward_conv(second_pad, last_out, extent)[0]
    denoised = volume.astype(jnp.float32) - residue
    chosen = jnp.take(measured, angle_ids, axis=1)
    forward_rays, cot_rays = project_pair(denoised, cotangent, ray_bins)
    weighted = curvature(forward_rays - chosen) * cot_rays
    grad_denoised = cotangent - 0.25 / ANG * back_project(weighted, ray_bins)
    grad_scale = float(NZ * NH * W) ** (-0.5)
    grad_last = (-grad_denoised)[None].astype(jnp.bfloat16)
    last_pad = pad_cells(grad_last)
    grad_kernel_out = kernel_grad(grad_last, second_pad, extent)[:, 0, :] * grad_scale
    grad_second = adjoint_conv(last_pad, last_out, extent)
    grad_mid = (grad_second * slope_second).astype(jnp.bfloat16)
    mid_pad = pad_cells(grad_mid)
    grad_kernel_mid = kernel_grad(grad_mid, first_pad, extent) * grad_scale
    grad_first = adjoint_conv(mid_pad, kernel_mid, extent)
    grad_low = (grad_first * slope_first).astype(jnp.bfloat16)
    low_pad = pad_cells(grad_low)
    grad_kernel_in = kernel_grad(grad_low, source_pad, extent)[:, :, 0] * grad_scale
    grad_volume = grad_denoised + adjoint_conv(low_pad, first_in, extent)[0]
    return (grad_volume, grad_kernel_in, grad_kernel_mid, grad_kernel_out)
```

```python
import functools

import numpy as np
import jax
import jax.numpy as jnp
from jax import lax
from jax.experimental import pallas as pl
from jax.experimental.pallas import tpu as pltpu
from jax.sharding import PartitionSpec as P

MESH = pl.DeviceIdType.MESH
BF = jnp.bfloat16
F32 = jnp.float32
DELTA = 6.0
VMEM_LIMIT = 56 * 1024 * 1024
NT = (((1,), (1,)), ((), ()))


def mm(a, b):
    return jnp.dot(a, b, preferred_element_type=F32)


def mm_nt(a, b):
    return lax.dot_general(a, b, NT, preferred_element_type=F32)


def shift(x, j):
    if j == 1:
        return x
    width = x.shape[-1]
    lane = lax.broadcasted_iota(jnp.int32, x.shape, x.ndim - 1)
    if j == 0:
        return jnp.where(lane == 0, 0.0, pltpu.roll(x, 1, x.ndim - 1))
    return jnp.where(lane == width - 1, 0.0, pltpu.roll(x, width - 1, x.ndim - 1))


def sig(v):
    return 1.0 / (1.0 + jnp.exp(-v))


def halo_targets(depth, plane):
    d, p = lax.axis_index("depth"), lax.axis_index("plane")
    out = []
    for dz in (-1, 0, 1):
        for dy in (-1, 0, 1):
            if dz == 0 and dy == 0:
                continue
            there = (d + dz >= 0) & (d + dz < depth) & (p + dy >= 0) & (p + dy < plane)
            out.append((dz, dy, there, (d + dz, p + dy)))
    return out


def halo_copy(dz, dy, who, mine, slots, send, recv):
    slot = (1 - dz) * 3 + (1 - dy)
    return pltpu.make_async_remote_copy(
        src_ref=mine, dst_ref=slots.at[slot], send_sem=send.at[slot], recv_sem=recv.at[slot],
        device_id=who, device_id_type=MESH)


def halo_start(targets, mine, slots, send, recv):
    for dz, dy, there, who in targets:
        @pl.when(there)
        def _(dz=dz, dy=dy, who=who):
            halo_copy(dz, dy, who, mine, slots, send, recv).start()


def halo_wait(targets, mine, slots, send, recv):
    for dz, dy, there, who in targets:
        @pl.when(there)
        def _(dz=dz, dy=dy, who=who):
            halo_copy(dz, dy, who, mine, slots, send, recv).wait_send()
            halo_copy(-dz, -dy, who, mine, slots, send, recv).wait_recv()


def halo_kernel(depth, plane, block, out, slots, send, recv):
    targets = halo_targets(depth, plane)
    slots[...] = jnp.zeros_like(slots)
    bar = pltpu.get_barrier_semaphore()
    count = jnp.int32(0)
    for _, _, there, who in targets:
        @pl.when(there)
        def _(who=who):
            pl.semaphore_signal(bar, inc=1, device_id=who, device_id_type=MESH)
        count = count + there.astype(jnp.int32)
    pl.semaphore_wait(bar, count)
    halo_start(targets, block, slots, send, recv)
    halo_wait(targets, block, slots, send, recv)
    out[...] = slots[...]
    out[4] = block[...]


def fill_shifts(sel, slots, dst):
    flat = slots[...].reshape(9 * 16, 128)
    wide = mm(sel[...], flat)
    for z in range(12):
        rows = wide[z * 16:(z + 1) * 16]
        for j in range(3):
            dst[z * 48 + j * 16:z * 48 + (j + 1) * 16, :] = shift(rows, j).astype(BF)
    return wide


def keep_rows(shape, z, margin, depth, plane):
    d, p = lax.axis_index("depth"), lax.axis_index("plane")
    gz = d * 4 + z - margin
    row = lax.broadcasted_iota(jnp.int32, shape, 0)
    low = (margin - p * 4) * 32
    high = (plane * 4 + margin - p * 4) * 32
    high = jnp.where((gz >= 0) & (gz < depth * 4), high, -1)
    return (row >= low) & (row < high)


def build_onehot(bins, a, c, size):
    parts = []
    for y in range(4):
        row = bins[pl.ds(a * 4 + y, 1), :]
        at = lax.broadcasted_iota(jnp.int32, (size, 128), 0) + c * size
        parts.append(jnp.where(at == row, 1.0, 0.0).astype(BF))
    return jnp.concatenate(parts, axis=1)


def forward_kernel(depth, plane, lanes, slots, sel, t1, w2, t3, selp, cot, bins,
                   s_out, r_out, slope1, slope2, a2, proj):
    wide = fill_shifts(sel, slots, s_out)
    for z in range(10):
        pre = mm(t1[...], s_out[z * 48:z * 48 + 144, :])
        sg = sig(pre)
        keep = keep_rows(pre.shape, z, 3, depth, plane)
        act = jnp.where(keep, pre * sg, 0.0)
        for j in range(3):
            moved = shift(act, j).astype(BF)
            for y in range(10):
                r_out[z, y * 96 + j * 32:y * 96 + j * 32 + 32, :] = moved[y * 32:y * 32 + 32]
        if 2 <= z < 8:
            slope = jnp.where(keep, sg * (1.0 + pre * (1.0 - sg)), 0.0)
            slope1[z - 2] = slope[64:256]
    for y in range(0, 8, 2):
        res = []
        for z in range(10):
            rhs = jnp.concatenate(
                [r_out[z, y * 96:y * 96 + 288, :], r_out[z, y * 96 + 96:y * 96 + 384, :]], axis=1)
            res.append(mm(w2[...], rhs))
        for z in range(8):
            pre2 = res[z][0:32] + res[z + 1][32:64] + res[z + 2][64:96]
            for q in range(2):
                yy = y + q
                pre = pre2[:, q * 128:q * 128 + 128]
                sg = sig(pre)
                keep = keep_rows((256, 128), z, 2, depth, plane)[yy * 32:yy * 32 + 32]
                slope2[z, yy * 32:yy * 32 + 32, :] = jnp.where(
                    keep, sg * (1.0 + pre * (1.0 - sg)), 0.0)
                if 1 <= z < 7 and 1 <= yy < 7:
                    a2[z - 1, (yy - 1) * 32:yy * 32, :] = jnp.where(keep, pre * sg, 0.0).astype(BF)
    den = []
    res = [mm(t3[...], a2[z]) for z in range(6)]
    for z in range(4):
        total = wide[(z + 4) * 16:(z + 4) * 16 + 8]
        for j in range(3):
            part = res[z][j * 24:j * 24 + 8] + res[z + 1][j * 24 + 8:j * 24 + 16] \
                + res[z + 2][j * 24 + 16:j * 24 + 24]
            total = total - shift(part, j)
        den.append(total)
    both = jnp.concatenate(den + [cot[...]], axis=0)
    high = both.astype(BF)
    rest = (both - high.astype(F32)).astype(BF)
    stacked = mm(selp[...], jnp.concatenate([high, rest], axis=0)).astype(BF)
    lhs = jnp.concatenate([stacked[y * 16:y * 16 + 16] for y in range(4)], axis=1)
    per = 512 // lanes

    def view(a, carry):
        halves = []
        for half in range(2):
            row = []
            for c in range(2):
                got = mm_nt(lhs, build_onehot(bins, a, half * 2 + c, 256))
                row.append(got[0:8] + got[8:16])
            halves.append(jnp.concatenate(row, axis=1))
        full = jnp.concatenate(halves, axis=0)
        for q in range(per):
            proj[a * per + q] = full[:, q * lanes:(q + 1) * lanes]
        return carry

    lax.fori_loop(0, 8, view, 0)


def rays_kernel(depth, plane, lanes, proj, chosen, bins, cot, sely, gd_out, out,
                onehot, got, mine, ag, block, slots, send1, recv1, send2, recv2, send3, recv3):
    d, p = lax.axis_index("depth"), lax.axis_index("plane")
    targets = halo_targets(depth, plane)
    slots[...] = jnp.zeros_like(slots)
    bar = pltpu.get_barrier_semaphore()
    count = jnp.int32(plane - 1)
    for i in range(1, plane):
        pl.semaphore_signal(bar, inc=1, device_id=(d, lax.rem(p + i, plane)), device_id_type=MESH)
    for dz, _, there, who in targets:
        if dz != 0:
            @pl.when(there)
            def _(who=who):
                pl.semaphore_signal(bar, inc=1, device_id=who, device_id_type=MESH)
            count = count + there.astype(jnp.int32)
    pl.semaphore_wait(bar, count)

    def first(i):
        to = lax.rem(p + i, plane)
        return pltpu.make_async_remote_copy(
            src_ref=proj.at[to], dst_ref=got.at[i], send_sem=send1.at[i], recv_sem=recv1.at[i],
            device_id=(d, to), device_id_type=MESH)

    def second(i):
        to = lax.rem(p + i, plane)
        return pltpu.make_async_remote_copy(
            src_ref=mine, dst_ref=ag.at[p], send_sem=send2.at[i], recv_sem=recv2.at[i],
            device_id=(d, to), device_id_type=MESH)

    for i in range(1, plane):
        first(i).start()

    def fill(k, carry):
        a = k // 4
        c = lax.rem(k, 4)
        onehot[pl.ds(pl.multiple_of(k * 256, 256), 256), :] = build_onehot(bins, a, c, 256)
        return carry

    lax.fori_loop(0, 32, fill, 0)
    total = proj[p]
    for i in range(1, plane):
        first(i).wait_recv()
        total = total + got[i]
    ratio = (total - chosen[p]) / DELTA
    inner = 1.0 + ratio * ratio
    weighted = pltpu.roll(total, 12, 0) / (inner * jnp.sqrt(inner))
    lead = weighted.astype(BF).astype(F32)
    row = lax.rem(lax.broadcasted_iota(jnp.int32, weighted.shape, 0), 8)
    mine[...] = jnp.where(row < 4, lead, pltpu.roll(weighted - lead, 4, 0)).astype(BF)
    for i in range(1, plane):
        second(i).start()
    for i in range(1, plane):
        second(i).wait_recv()
        first(i).wait_send()
    for i in range(1, plane):
        second(i).wait_send()
    ag[p] = mine[...]
    per = 512 // lanes
    low = jnp.zeros((16, 512), F32)
    up = jnp.zeros((16, 512), F32)
    for a in range(8):
        lhs = jnp.concatenate([ag[a * per + q] for q in range(per)], axis=1)
        low = low + mm(lhs, onehot[a * 1024:a * 1024 + 512, :])
        up = up + mm(lhs, onehot[a * 1024 + 512:a * 1024 + 1024, :])
    up = pltpu.roll(up, 8, 0)
    back = low + up
    back = back + pltpu.roll(back, 12, 0)
    row = lax.broadcasted_iota(jnp.int32, (16, 512), 0)
    gd = jnp.where(row < 4, cot[...] - back * (0.25 / 8), 0.0)
    gd_out[...] = gd
    neg = (-gd).astype(BF)
    total = jnp.zeros((16, 128), F32)
    for y in range(4):
        total = total + mm(sely[y], neg[:, y * 128:y * 128 + 128])
    block[...] = total.astype(BF)
    halo_start(targets, block, slots, send3, recv3)
    halo_wait(targets, block, slots, send3, recv3)
    out[...] = slots[...]
    out[4] = block[...]


def backward_kernel(slots, sel, t4, w2, t5, s, r, slope1, slope2, a2,
                    adj, terms, sg, rm, gl):
    fill_shifts(sel, slots, sg)
    for z in range(8):
        grad = mm(t4[...], sg[(z + 1) * 48:(z + 1) * 48 + 144, :]) * slope2[z]
        for j in range(3):
            moved = shift(grad, j).astype(BF)
            for y in range(8):
                rm[z, y * 96 + j * 32:y * 96 + j * 32 + 32, :] = moved[y * 32:y * 32 + 32]
    for y in range(0, 6, 2):
        res = []
        for z in range(8):
            rhs = jnp.concatenate(
                [rm[z, y * 96:y * 96 + 288, :], rm[z, y * 96 + 96:y * 96 + 384, :]], axis=1)
            res.append(mm(w2[...], rhs))
        for z in range(6):
            grad = res[z][0:32] + res[z + 1][32:64] + res[z + 2][64:96]
            for q in range(2):
                yy = y + q
                at = slice(yy * 32, yy * 32 + 32)
                gl[z, at, :] = (grad[:, q * 128:q * 128 + 128] * slope1[z, at, :]).astype(BF)
    res = [mm(t5[...], gl[z]) for z in range(6)]
    for z in range(4):
        total = jnp.zeros((8, 128), F32)
        for j in range(3):
            part = res[z][j * 24:j * 24 + 8] + res[z + 1][j * 24 + 8:j * 24 + 16] \
                + res[z + 2][j * 24 + 16:j * 24 + 24]
            total = total + shift(part, j)
        adj[z] = total
    mid = jnp.zeros((288, 96), F32)
    none = jnp.zeros((32, 512), BF)
    own = [
        jnp.concatenate(
            [rm[z + 2, (y + 2) * 96 + 32:(y + 2) * 96 + 64, :] for y in range(4)], axis=1)
        for z in range(4)
    ]
    for t in range(6):
        lhs = jnp.concatenate(
            [r[t + 2, (y + 2) * 96:(y + 2) * 96 + 288, :] for y in range(4)], axis=1)
        rhs = jnp.concatenate(
            [own[t - j] if 0 <= t - j < 4 else none for j in range(3)], axis=0)
        mid = mid + mm_nt(lhs, rhs)
    terms[...] = jnp.zeros_like(terms)
    terms[0:288, 0:96] = mid
    first = jnp.zeros((144, 128), F32)
    for z in range(4):
        first = first + mm_nt(s[(z + 3) * 48:(z + 3) * 48 + 144, :], gl[z + 1, 32:160, :])
    third = jnp.zeros((144, 192), F32)
    blank = jnp.zeros((48, 128), BF)
    for t in range(6):
        lhs = jnp.concatenate(
            [sg[(4 + t - j) * 48:(5 + t - j) * 48, :] if 0 <= t - j < 4 else blank
             for j in range(3)], axis=0)
        third = third + mm_nt(lhs, a2[t])
    third = jnp.concatenate([third, jnp.zeros((144, 64), F32)], axis=1)
    row = lax.rem(lax.broadcasted_iota(jnp.int32, (144, 128), 0), 16)
    group = lax.broadcasted_iota(jnp.int32, (144, 128), 1) // 32
    for jy in range(3):
        pick = jnp.where(row == group + (3 + jy), first, 0.0).reshape(9, 16, 128).sum(axis=1)
        terms[288 + jy * 16:288 + jy * 16 + 16, :] = jnp.concatenate(
            [pick, jnp.zeros((7, 128), F32)], axis=0)
        own_row = (row >= 4) & (row < 8)
        pick = jnp.where(own_row & (row - 4 + jy == group), third[:, 0:128], 0.0) \
            + jnp.where(own_row & (row - 4 + jy == group + 4), third[:, 128:256], 0.0)
        pick = pick.reshape(9, 16, 128).sum(axis=1)
        terms[336 + jy * 16:336 + jy * 16 + 16, :] = jnp.concatenate(
            [pick, jnp.zeros((7, 128), F32)], axis=0)


def sum_kernel(depth, plane, terms, out, got, part, other, mine, ag, s1, r1, s2, r2, s3, r3):
    d, p = lax.axis_index("depth"), lax.axis_index("plane")
    bar = pltpu.get_barrier_semaphore()
    for i in range(1, plane):
        pl.semaphore_signal(bar, inc=1, device_id=(d, lax.rem(p + i, plane)), device_id_type=MESH)
    for i in range(1, depth):
        pl.semaphore_signal(bar, inc=1, device_id=(lax.rem(d + i, depth), p), device_id_type=MESH)
    pl.semaphore_wait(bar, plane + depth - 2)

    def first(i):
        to = lax.rem(p + i, plane)
        return pltpu.make_async_remote_copy(
            src_ref=terms.at[to], dst_ref=got.at[i], send_sem=s1.at[i], recv_sem=r1.at[i],
            device_id=(d, to), device_id_type=MESH)

    def second(i):
        return pltpu.make_async_remote_copy(
            src_ref=part, dst_ref=other.at[i], send_sem=s2.at[i], recv_sem=r2.at[i],
            device_id=(lax.rem(d + i, depth), p), device_id_type=MESH)

    def third(i):
        return pltpu.make_async_remote_copy(
            src_ref=mine, dst_ref=ag.at[p], send_sem=s3.at[i], recv_sem=r3.at[i],
            device_id=(d, lax.rem(p + i, plane)), device_id_type=MESH)

    for i in range(1, plane):
        first(i).start()
    total = terms[p].astype(F32)
    for i in range(1, plane):
        first(i).wait_recv()
        total = total + got[i].astype(F32)
    part[...] = total
    for i in range(1, depth):
        second(i).start()
    for i in range(1, depth):
        second(i).wait_recv()
    other[0] = total
    total = jnp.zeros_like(total)
    for k in range(depth):
        total = total + other[lax.rem(d - k + depth, depth)]
    mine[...] = total.astype(BF)
    for i in range(1, plane):
        third(i).start()
    for i in range(1, plane):
        third(i).wait_recv()
        first(i).wait_send()
        third(i).wait_send()
    for i in range(1, depth):
        second(i).wait_send()
    ag[p] = mine[...]
    out[...] = ag[...].astype(F32)


def tall(kernel, rows, off):
    where = np.zeros((3, rows, 16), np.float32)
    for jy in range(3):
        for y in range(rows):
            where[jy, y, y + off + jy - 1] = 1.0
    k = kernel.reshape(3, 3, 3, -1)
    full = jnp.einsum("zyxc,yab->aczxb", k, jnp.asarray(where, BF), preferred_element_type=F32)
    return full.reshape(rows * k.shape[3], 144).astype(BF)


def flat(kernel):
    where = np.zeros((3, 8, 6), np.float32)
    for jy in range(3):
        for y in range(4):
            where[jy, y + 4, y + jy] = 1.0
    k = kernel.reshape(3, 3, 3, -1)
    full = jnp.einsum("zyxc,yab->xzabc", k, jnp.asarray(where, BF), preferred_element_type=F32)
    return full.reshape(72, 6 * k.shape[3]).astype(BF)


def square(kernel):
    o, c = kernel.shape[1:]
    k = kernel.reshape(3, 3, 3, o, c)
    return k.transpose(0, 3, 1, 2, 4).reshape(3 * o, 9 * c)


def selectors():
    sel = np.zeros((192, 144), np.float32)
    for z in range(12):
        for y in range(12):
            sel[z * 16 + y, ((z // 4) * 3 + y // 4) * 16 + (z % 4) * 4 + y % 4] = 1.0
    selp = np.zeros((64, 96), np.float32)
    for y in range(4):
        for z in range(4):
            for k in range(2):
                selp[y * 16 + k * 8 + z, k * 48 + z * 8 + 4 + y] = 1.0
                selp[y * 16 + k * 8 + 4 + z, k * 48 + 32 + z * 4 + y] = 1.0
    sely = np.zeros((4, 16, 16), np.float32)
    for y in range(4):
        for z in range(4):
            sely[y, z * 4 + y, z] = 1.0
    return [jnp.asarray(x, BF) for x in (sel, selp, sely)]


def call(body, outs, scratch, args, cid=None):
    vm = pl.BlockSpec(memory_space=pltpu.VMEM)
    extra = {} if cid is None else dict(collective_id=cid, has_side_effects=True)
    return pl.pallas_call(
        body,
        out_shape=[jax.ShapeDtypeStruct(s, t) for s, t in outs],
        in_specs=[vm] * len(args),
        out_specs=[vm] * len(outs),
        scratch_shapes=scratch,
        compiler_params=pltpu.CompilerParams(vmem_limit_bytes=VMEM_LIMIT, **extra),
    )(*args)


def per_device(volume, cotangent, kernel_in, kernel_mid, kernel_out, measured, angle_ids, ray_bins):
    depth, plane = lax.axis_size("depth"), lax.axis_size("plane")
    nz, nh, width = volume.shape
    chan = kernel_in.shape[1]
    sem = pltpu.SemaphoreType.DMA
    sel, selp, sely = selectors()
    lanes = 8 * 512 // plane
    per = 512 // lanes
    bins = ray_bins.reshape(32, 128)
    t1 = tall(kernel_in, 10, 1)
    t4 = tall(kernel_out[::-1], 8, 2)
    t3 = flat(kernel_out)
    t5 = flat(kernel_in[::-1])
    w2f = square(kernel_mid)
    w2b = square(kernel_mid[::-1].transpose(0, 2, 1))
    chosen = jnp.take(measured, angle_ids, axis=1)
    chosen = chosen.reshape(4, 8, 2, per, lanes).transpose(1, 3, 2, 0, 4)
    chosen = jnp.pad(chosen, ((0, 0), (0, 0), (0, 0), (0, 4), (0, 0))).reshape(plane, 16, lanes)

    vol_slots = call(
        functools.partial(halo_kernel, depth, plane), [((9, 16, 128), BF)],
        [pltpu.VMEM((9, 16, 128), BF), sem((9,)), sem((9,))],
        [volume.reshape(16, 128)], 0)[0]
    s, r, slope1, slope2, a2, proj = call(
        functools.partial(forward_kernel, depth, plane, lanes),
        [((576, 128), BF), ((10, 960, 128), BF), ((6, 192, 128), F32), ((8, 256, 128), F32),
         ((6, 192, 128), BF), ((plane, 16, lanes), F32)],
        [], [vol_slots, sel, t1, w2f, t3, selp, cotangent.reshape(16, 128), bins])
    cot_rows = jnp.pad(cotangent.reshape(4, 512), ((0, 12), (0, 0)))
    gd, grad_slots = call(
        functools.partial(rays_kernel, depth, plane, lanes),
        [((16, 512), F32), ((9, 16, 128), BF)],
        [pltpu.VMEM((8192, 512), BF), pltpu.VMEM((plane, 16, lanes), F32),
         pltpu.VMEM((16, lanes), BF), pltpu.VMEM((plane, 16, lanes), BF),
         pltpu.VMEM((16, 128), BF), pltpu.VMEM((9, 16, 128), BF),
         sem((plane,)), sem((plane,)), sem((plane,)), sem((plane,)), sem((9,)), sem((9,))],
        [proj, chosen, bins, cot_rows, sely], 1)
    chunk = 16 * plane
    rows = -(-384 // chunk) * chunk
    adj, terms = call(
        backward_kernel, [((4, 8, 128), F32), ((rows, 128), F32)],
        [pltpu.VMEM((576, 128), BF), pltpu.VMEM((8, 768, 128), BF), pltpu.VMEM((6, 192, 128), BF)],
        [grad_slots, sel, t4, w2b, t5, s, r, slope1, slope2, a2])
    each = rows // plane
    summed = call(
        functools.partial(sum_kernel, depth, plane), [((plane, each, 128), F32)],
        [pltpu.VMEM((plane, each, 128), F32), pltpu.VMEM((each, 128), F32),
         pltpu.VMEM((depth, each, 128), F32), pltpu.VMEM((each, 128), BF),
         pltpu.VMEM((plane, each, 128), BF),
         sem((plane,)), sem((plane,)), sem((depth,)), sem((depth,)), sem((plane,)), sem((plane,))],
        [terms.reshape(plane, each, 128)], 2)[0].reshape(rows, 128)
    scale = float(nz * depth * nh * plane * width) ** -0.5
    grad_volume = gd[:4].reshape(4, 4, 128) + adj[:, 4:8, :]
    mid = summed[:288, :96].reshape(3, 3, chan, 3, chan).transpose(3, 0, 1, 4, 2)
    mid = mid.reshape(27, chan, chan)
    small = summed[288:384].reshape(2, 3, 16, 4, chan).sum(axis=3)[:, :, :9]
    small = small.reshape(2, 3, 3, 3, chan).transpose(0, 2, 1, 3, 4)
    first = small[0].reshape(27, chan)
    third = small[1][:, :, ::-1].reshape(27, chan)
    return (grad_volume, first * scale, mid * scale, third * scale)


def solution(mesh):
    placed = (
        P("depth", "plane", None),
        P("depth", "plane", None),
        P(),
        P(),
        P(),
        P("depth", None, None),
        P(),
        P(None, "plane", None),
    )
    return jax.shard_map(
        per_device,
        mesh=mesh,
        in_specs=placed,
        out_specs=(P("depth", "plane", None), P(), P(), P()),
        check_vma=False,
    )
```

```python
import functools

import numpy as np
import jax
import jax.numpy as jnp
from jax import lax
from jax.experimental import pallas as pl
from jax.experimental.pallas import tpu as pltpu
from jax.sharding import PartitionSpec as P

MESH = pl.DeviceIdType.MESH
BF = jnp.bfloat16
F32 = jnp.float32
DELTA = 6.0
VMEM_LIMIT = 56 * 1024 * 1024
NT = (((1,), (1,)), ((), ()))


def mm(a, b):
    return jnp.dot(a, b, preferred_element_type=F32)


def mm_nt(a, b):
    return lax.dot_general(a, b, NT, preferred_element_type=F32)


def shift(x, j):
    if j == 1:
        return x
    width = x.shape[-1]
    lane = lax.broadcasted_iota(jnp.int32, x.shape, x.ndim - 1)
    if j == 0:
        return jnp.where(lane == 0, 0.0, pltpu.roll(x, 1, x.ndim - 1))
    return jnp.where(lane == width - 1, 0.0, pltpu.roll(x, width - 1, x.ndim - 1))


def sig(v):
    return 1.0 / (1.0 + jnp.exp(-v))


def halo_targets(depth, plane):
    d, p = lax.axis_index("depth"), lax.axis_index("plane")
    out = []
    for dz in (-1, 0, 1):
        for dy in (-1, 0, 1):
            if dz == 0 and dy == 0:
                continue
            there = (d + dz >= 0) & (d + dz < depth) & (p + dy >= 0) & (p + dy < plane)
            out.append((dz, dy, there, (d + dz, p + dy)))
    return out


def halo_copy(dz, dy, who, mine, slots, send, recv):
    slot = (1 - dz) * 3 + (1 - dy)
    return pltpu.make_async_remote_copy(
        src_ref=mine, dst_ref=slots.at[slot], send_sem=send.at[slot], recv_sem=recv.at[slot],
        device_id=who, device_id_type=MESH)


def halo_start(targets, mine, slots, send, recv):
    for dz, dy, there, who in targets:
        @pl.when(there)
        def _(dz=dz, dy=dy, who=who):
            halo_copy(dz, dy, who, mine, slots, send, recv).start()


def halo_wait(targets, mine, slots, send, recv):
    for dz, dy, there, who in targets:
        @pl.when(there)
        def _(dz=dz, dy=dy, who=who):
            halo_copy(dz, dy, who, mine, slots, send, recv).wait_send()
            halo_copy(-dz, -dy, who, mine, slots, send, recv).wait_recv()


def iota(shape, dim):
    return lax.broadcasted_iota(jnp.int32, shape, dim)


def ones_where(mask):
    return jnp.where(mask, 1.0, 0.0).astype(BF)


def tall(k, rows, off, flip):
    chan = k.shape[1]
    pick = ones_where(lax.rem(iota((rows * chan, chan), 0), chan) == iota((rows * chan, chan), 1))
    wide = mm_nt(pick, k).astype(BF)
    shape = (rows * chan, 144)
    y_in = lax.rem(iota(shape, 1), 16)
    y = iota(shape, 0) // chan
    col = iota((27, 144), 1)
    total = jnp.zeros(shape, F32)
    for jy in range(3):
        src = (col // 48) * 9 + jy * 3 + lax.rem(col // 16, 3)
        if flip:
            src = 26 - src
        part = mm(wide, ones_where(iota((27, 144), 0) == src))
        total = total + jnp.where(y_in == y + (off + jy - 1), part, 0.0)
    return total.astype(BF)


def flat(k, flip):
    chan = k.shape[1]
    shape = (72, 6 * chan)
    y = lax.rem(iota(shape, 0), 8)
    y_in = iota(shape, 1) // chan
    spread = ones_where(lax.rem(iota((chan, 6 * chan), 1), chan) == iota((chan, 6 * chan), 0))
    row = iota((72, 27), 0)
    total = jnp.zeros(shape, F32)
    for jy in range(3):
        src = lax.rem(row // 8, 3) * 9 + jy * 3 + row // 24
        if flip:
            src = 26 - src
        part = mm(mm(ones_where(iota((72, 27), 1) == src), k).astype(BF), spread)
        total = total + jnp.where((y >= 4) & (y_in == y - 4 + jy), part, 0.0)
    return total.astype(BF)


def square(k):
    chan = k.shape[1]
    total = jnp.zeros((3 * chan, 9 * chan), F32)
    for q in range(9):
        rows = jnp.concatenate([k[j * 9 + q] for j in range(3)], axis=0)
        place = ones_where(iota((chan, 9 * chan), 1) == iota((chan, 9 * chan), 0) + q * chan)
        total = total + mm(rows, place)
    return total.astype(BF)


def square_back(k):
    chan = k.shape[1]
    eye = ones_where(iota((chan, chan), 0) == iota((chan, chan), 1))
    return jnp.concatenate(
        [mm_nt(eye, jnp.concatenate([k[26 - j * 9 - q] for q in range(9)], axis=0))
         for j in range(3)], axis=0).astype(BF)


def fill_shifts(sel, slots, dst):
    flat = slots[...].reshape(9 * 16, 128)
    wide = mm(sel[...], flat)
    for z in range(12):
        rows = wide[z * 16:(z + 1) * 16]
        for j in range(3):
            dst[z * 48 + j * 16:z * 48 + (j + 1) * 16, :] = shift(rows, j).astype(BF)
    return wide


def keep_rows(shape, z, margin, depth, plane):
    d, p = lax.axis_index("depth"), lax.axis_index("plane")
    gz = d * 4 + z - margin
    row = lax.broadcasted_iota(jnp.int32, shape, 0)
    low = (margin - p * 4) * 32
    high = (plane * 4 + margin - p * 4) * 32
    high = jnp.where((gz >= 0) & (gz < depth * 4), high, -1)
    return (row >= low) & (row < high)


def build_onehot(bins, a, c, size):
    parts = []
    for y in range(4):
        row = bins[pl.ds(a * 4 + y, 1), :]
        at = lax.broadcasted_iota(jnp.int32, (size, 128), 0) + c * size
        parts.append(jnp.where(at == row, 1.0, 0.0).astype(BF))
    return jnp.concatenate(parts, axis=1)


def forward_kernel(depth, plane, lanes, block, sel, k1, k2, k3, selp, cot, bins,
                   s_out, r_out, slope1, slope2, a2, proj,
                   slots, t1, w2, t3, send, recv):
    targets = halo_targets(depth, plane)
    slots[...] = jnp.zeros_like(slots)
    bar = pltpu.get_barrier_semaphore()
    count = jnp.int32(0)
    for _, _, there, who in targets:
        @pl.when(there)
        def _(who=who):
            pl.semaphore_signal(bar, inc=1, device_id=who, device_id_type=MESH)
        count = count + there.astype(jnp.int32)
    pl.semaphore_wait(bar, count)
    halo_start(targets, block, slots, send, recv)
    t1[...] = tall(k1[...], 10, 1, False)
    w2[...] = square(k2)
    t3[...] = flat(k3[...], False)
    halo_wait(targets, block, slots, send, recv)
    slots[4] = block[...]
    wide = fill_shifts(sel, slots, s_out)
    for z in range(10):
        pre = mm(t1[...], s_out[z * 48:z * 48 + 144, :])
        sg = sig(pre)
        keep = keep_rows(pre.shape, z, 3, depth, plane)
        act = jnp.where(keep, pre * sg, 0.0)
        for j in range(3):
            moved = shift(act, j).astype(BF)
            for y in range(10):
                r_out[z, y * 96 + j * 32:y * 96 + j * 32 + 32, :] = moved[y * 32:y * 32 + 32]
        if 2 <= z < 8:
            slope = jnp.where(keep, sg * (1.0 + pre * (1.0 - sg)), 0.0)
            slope1[z - 2] = slope[64:256]
    for y in range(0, 8, 2):
        res = []
        for z in range(10):
            rhs = jnp.concatenate(
                [r_out[z, y * 96:y * 96 + 288, :], r_out[z, y * 96 + 96:y * 96 + 384, :]], axis=1)
            res.append(mm(w2[...], rhs))
        for z in range(8):
            pre2 = res[z][0:32] + res[z + 1][32:64] + res[z + 2][64:96]
            for q in range(2):
                yy = y + q
                pre = pre2[:, q * 128:q * 128 + 128]
                sg = sig(pre)
                keep = keep_rows((256, 128), z, 2, depth, plane)[yy * 32:yy * 32 + 32]
                slope2[z, yy * 32:yy * 32 + 32, :] = jnp.where(
                    keep, sg * (1.0 + pre * (1.0 - sg)), 0.0)
                if 1 <= z < 7 and 1 <= yy < 7:
                    a2[z - 1, (yy - 1) * 32:yy * 32, :] = jnp.where(keep, pre * sg, 0.0).astype(BF)
    den = []
    res = [mm(t3[...], a2[z]) for z in range(6)]
    for z in range(4):
        total = wide[(z + 4) * 16:(z + 4) * 16 + 8]
        for j in range(3):
            part = res[z][j * 24:j * 24 + 8] + res[z + 1][j * 24 + 8:j * 24 + 16] \
                + res[z + 2][j * 24 + 16:j * 24 + 24]
            total = total - shift(part, j)
        den.append(total)
    both = jnp.concatenate(den + [cot[...]], axis=0)
    high = both.astype(BF)
    rest = (both - high.astype(F32)).astype(BF)
    stacked = mm(selp[...], jnp.concatenate([high, rest], axis=0)).astype(BF)
    lhs = jnp.concatenate([stacked[y * 16:y * 16 + 16] for y in range(4)], axis=1)
    per = 512 // lanes

    def view(a, carry):
        halves = []
        for half in range(2):
            row = []
            for c in range(2):
                got = mm_nt(lhs, build_onehot(bins, a, half * 2 + c, 256))
                row.append(got[0:8] + got[8:16])
            halves.append(jnp.concatenate(row, axis=1))
        full = jnp.concatenate(halves, axis=0)
        for q in range(per):
            proj[a * per + q] = full[:, q * lanes:(q + 1) * lanes]
        return carry

    lax.fori_loop(0, 8, view, 0)


def rays_kernel(depth, plane, lanes, proj, chosen, bins, cot, sely, k1, k2, k3,
                gd_out, out, t4, w2, t5,
                onehot, got, mine, ag, block, slots, send1, recv1, send2, recv2, send3, recv3):
    d, p = lax.axis_index("depth"), lax.axis_index("plane")
    targets = halo_targets(depth, plane)
    slots[...] = jnp.zeros_like(slots)
    bar = pltpu.get_barrier_semaphore()
    count = jnp.int32(plane - 1)
    for i in range(1, plane):
        pl.semaphore_signal(bar, inc=1, device_id=(d, lax.rem(p + i, plane)), device_id_type=MESH)
    for dz, _, there, who in targets:
        if dz != 0:
            @pl.when(there)
            def _(who=who):
                pl.semaphore_signal(bar, inc=1, device_id=who, device_id_type=MESH)
            count = count + there.astype(jnp.int32)
    pl.semaphore_wait(bar, count)

    def first(i):
        to = lax.rem(p + i, plane)
        return pltpu.make_async_remote_copy(
            src_ref=proj.at[to], dst_ref=got.at[i], send_sem=send1.at[i], recv_sem=recv1.at[i],
            device_id=(d, to), device_id_type=MESH)

    def second(i):
        to = lax.rem(p + i, plane)
        return pltpu.make_async_remote_copy(
            src_ref=mine, dst_ref=ag.at[p], send_sem=send2.at[i], recv_sem=recv2.at[i],
            device_id=(d, to), device_id_type=MESH)

    for i in range(1, plane):
        first(i).start()

    def fill(k, carry):
        a = k // 4
        c = lax.rem(k, 4)
        onehot[pl.ds(pl.multiple_of(k * 256, 256), 256), :] = build_onehot(bins, a, c, 256)
        return carry

    lax.fori_loop(0, 32, fill, 0)
    t4[...] = tall(k3[...], 8, 2, True)
    w2[...] = square_back(k2)
    t5[...] = flat(k1[...], True)
    total = proj[p]
    for i in range(1, plane):
        first(i).wait_recv()
        total = total + got[i]
    ratio = (total - chosen[p]) / DELTA
    inner = 1.0 + ratio * ratio
    weighted = pltpu.roll(total, 12, 0) / (inner * jnp.sqrt(inner))
    lead = weighted.astype(BF).astype(F32)
    row = lax.rem(lax.broadcasted_iota(jnp.int32, weighted.shape, 0), 8)
    mine[...] = jnp.where(row < 4, lead, pltpu.roll(weighted - lead, 4, 0)).astype(BF)
    for i in range(1, plane):
        second(i).start()
    for i in range(1, plane):
        second(i).wait_recv()
        first(i).wait_send()
    for i in range(1, plane):
        second(i).wait_send()
    ag[p] = mine[...]
    per = 512 // lanes
    low = jnp.zeros((16, 512), F32)
    up = jnp.zeros((16, 512), F32)
    for a in range(8):
        lhs = jnp.concatenate([ag[a * per + q] for q in range(per)], axis=1)
        low = low + mm(lhs, onehot[a * 1024:a * 1024 + 512, :])
        up = up + mm(lhs, onehot[a * 1024 + 512:a * 1024 + 1024, :])
    up = pltpu.roll(up, 8, 0)
    back = low + up
    back = back + pltpu.roll(back, 12, 0)
    row = lax.broadcasted_iota(jnp.int32, (16, 512), 0)
    gd = jnp.where(row < 4, cot[...] - back * (0.25 / 8), 0.0)
    gd_out[...] = gd
    neg = (-gd).astype(BF)
    total = jnp.zeros((16, 128), F32)
    for y in range(4):
        total = total + mm(sely[y], neg[:, y * 128:y * 128 + 128])
    block[...] = total.astype(BF)
    halo_start(targets, block, slots, send3, recv3)
    halo_wait(targets, block, slots, send3, recv3)
    out[...] = slots[...]
    out[4] = block[...]


def backward_kernel(depth, plane, scale, slots, sel, t4, w2, t5, s, r, slope1, slope2, a2,
                    adj, out1, out2, out3, terms, sg, rm, gl,
                    got, part, other, mine, ag, s1, r1, s2, r2, s3, r3):
    d, p = lax.axis_index("depth"), lax.axis_index("plane")
    bar = pltpu.get_barrier_semaphore()
    for i in range(1, plane):
        pl.semaphore_signal(bar, inc=1, device_id=(d, lax.rem(p + i, plane)), device_id_type=MESH)
    for i in range(1, depth):
        pl.semaphore_signal(bar, inc=1, device_id=(lax.rem(d + i, depth), p), device_id_type=MESH)
    fill_shifts(sel, slots, sg)
    for z in range(8):
        grad = mm(t4[...], sg[(z + 1) * 48:(z + 1) * 48 + 144, :]) * slope2[z]
        for j in range(3):
            moved = shift(grad, j).astype(BF)
            for y in range(8):
                rm[z, y * 96 + j * 32:y * 96 + j * 32 + 32, :] = moved[y * 32:y * 32 + 32]
    for y in range(0, 6, 2):
        res = []
        for z in range(8):
            rhs = jnp.concatenate(
                [rm[z, y * 96:y * 96 + 288, :], rm[z, y * 96 + 96:y * 96 + 384, :]], axis=1)
            res.append(mm(w2[...], rhs))
        for z in range(6):
            grad = res[z][0:32] + res[z + 1][32:64] + res[z + 2][64:96]
            for q in range(2):
                yy = y + q
                at = slice(yy * 32, yy * 32 + 32)
                gl[z, at, :] = (grad[:, q * 128:q * 128 + 128] * slope1[z, at, :]).astype(BF)
    res = [mm(t5[...], gl[z]) for z in range(6)]
    for z in range(4):
        total = jnp.zeros((8, 128), F32)
        for j in range(3):
            piece = res[z][j * 24:j * 24 + 8] + res[z + 1][j * 24 + 8:j * 24 + 16] \
                + res[z + 2][j * 24 + 16:j * 24 + 24]
            total = total + shift(piece, j)
        adj[z] = total
    mid = jnp.zeros((288, 96), F32)
    none = jnp.zeros((32, 512), BF)
    own = [
        jnp.concatenate(
            [rm[z + 2, (y + 2) * 96 + 32:(y + 2) * 96 + 64, :] for y in range(4)], axis=1)
        for z in range(4)
    ]
    for t in range(6):
        lhs = jnp.concatenate(
            [r[t + 2, (y + 2) * 96:(y + 2) * 96 + 288, :] for y in range(4)], axis=1)
        rhs = jnp.concatenate(
            [own[t - j] if 0 <= t - j < 4 else none for j in range(3)], axis=0)
        mid = mid + mm_nt(lhs, rhs)
    terms[...] = jnp.zeros_like(terms)
    terms[0:288, 0:96] = mid
    first = jnp.zeros((144, 128), F32)
    for z in range(4):
        first = first + mm_nt(s[(z + 3) * 48:(z + 3) * 48 + 144, :], gl[z + 1, 32:160, :])
    third = jnp.zeros((144, 192), F32)
    blank = jnp.zeros((48, 128), BF)
    for t in range(6):
        lhs = jnp.concatenate(
            [sg[(4 + t - j) * 48:(5 + t - j) * 48, :] if 0 <= t - j < 4 else blank
             for j in range(3)], axis=0)
        third = third + mm_nt(lhs, a2[t])
    third = jnp.concatenate([third, jnp.zeros((144, 64), F32)], axis=1)
    row = lax.rem(lax.broadcasted_iota(jnp.int32, (144, 128), 0), 16)
    group = lax.broadcasted_iota(jnp.int32, (144, 128), 1) // 32
    for jy in range(3):
        pick = jnp.where(row == group + (3 + jy), first, 0.0).reshape(9, 16, 128).sum(axis=1)
        terms[288 + jy * 16:288 + jy * 16 + 16, :] = jnp.concatenate(
            [pick, jnp.zeros((7, 128), F32)], axis=0)
        own_row = (row >= 4) & (row < 8)
        pick = jnp.where(own_row & (row - 4 + jy == group), third[:, 0:128], 0.0) \
            + jnp.where(own_row & (row - 4 + jy == group + 4), third[:, 128:256], 0.0)
        pick = pick.reshape(9, 16, 128).sum(axis=1)
        terms[336 + jy * 16:336 + jy * 16 + 16, :] = jnp.concatenate(
            [pick, jnp.zeros((7, 128), F32)], axis=0)
    pl.semaphore_wait(bar, plane + depth - 2)
    each = terms.shape[0] // plane

    def rows_of(q):
        return terms.at[pl.ds(pl.multiple_of(q * each, each), each)]

    def first(i):
        to = lax.rem(p + i, plane)
        return pltpu.make_async_remote_copy(
            src_ref=rows_of(to), dst_ref=got.at[i], send_sem=s1.at[i], recv_sem=r1.at[i],
            device_id=(d, to), device_id_type=MESH)

    def second(i):
        return pltpu.make_async_remote_copy(
            src_ref=part, dst_ref=other.at[i], send_sem=s2.at[i], recv_sem=r2.at[i],
            device_id=(lax.rem(d + i, depth), p), device_id_type=MESH)

    def third(i):
        return pltpu.make_async_remote_copy(
            src_ref=mine, dst_ref=ag.at[p], send_sem=s3.at[i], recv_sem=r3.at[i],
            device_id=(d, lax.rem(p + i, plane)), device_id_type=MESH)

    for i in range(1, plane):
        first(i).start()
    total = rows_of(p)[...]
    for i in range(1, plane):
        first(i).wait_recv()
        total = total + got[i]
    part[...] = total
    for i in range(1, depth):
        second(i).start()
    for i in range(1, depth):
        second(i).wait_recv()
    other[0] = total
    total = jnp.zeros_like(total)
    for k in range(depth):
        total = total + other[lax.rem(d - k + depth, depth)]
    mine[...] = total.astype(BF)
    for i in range(1, plane):
        third(i).start()
    for i in range(1, plane):
        third(i).wait_recv()
        first(i).wait_send()
        third(i).wait_send()
    for i in range(1, depth):
        second(i).wait_send()
    ag[p] = mine[...]
    summed = ag[...].reshape(plane * each, 128)
    chan = out2.shape[1]
    for j in range(3):
        pick = ones_where(iota((chan, 128), 1) == iota((chan, 128), 0) + j * chan)
        for q in range(9):
            out2[j * 9 + q] = mm_nt(pick, summed[q * chan:(q + 1) * chan]) * scale
    fold = ones_where(lax.rem(iota((128, chan), 0), chan) == iota((128, chan), 1))
    k = iota((32, 48), 0)
    for at, flip, out in ((288, False, out1), (336, True, out3)):
        jx = lax.rem(k, 3)
        jx = 2 - jx if flip else jx
        order = ones_where(iota((32, 48), 1) == lax.rem(k // 3, 3) * 16 + (k // 9) * 3 + jx)
        moved = mm(order, summed[at:at + 48]).astype(BF)
        out[...] = mm(moved, fold)[0:27] * scale


def selectors():
    sel = np.zeros((192, 144), np.float32)
    for z in range(12):
        for y in range(12):
            sel[z * 16 + y, ((z // 4) * 3 + y // 4) * 16 + (z % 4) * 4 + y % 4] = 1.0
    selp = np.zeros((64, 96), np.float32)
    for y in range(4):
        for z in range(4):
            for k in range(2):
                selp[y * 16 + k * 8 + z, k * 48 + z * 8 + 4 + y] = 1.0
                selp[y * 16 + k * 8 + 4 + z, k * 48 + 32 + z * 4 + y] = 1.0
    sely = np.zeros((4, 16, 16), np.float32)
    for y in range(4):
        for z in range(4):
            sely[y, z * 4 + y, z] = 1.0
    return [jnp.asarray(x, BF) for x in (sel, selp, sely)]


def call(body, outs, scratch, args, cid=None):
    vm = pl.BlockSpec(memory_space=pltpu.VMEM)
    extra = {} if cid is None else dict(collective_id=cid, has_side_effects=True)
    return pl.pallas_call(
        body,
        out_shape=[jax.ShapeDtypeStruct(s, t) for s, t in outs],
        in_specs=[vm] * len(args),
        out_specs=[vm] * len(outs),
        scratch_shapes=scratch,
        compiler_params=pltpu.CompilerParams(vmem_limit_bytes=VMEM_LIMIT, **extra),
    )(*args)


def per_device(volume, cotangent, kernel_in, kernel_mid, kernel_out, measured, angle_ids, ray_bins):
    depth, plane = lax.axis_size("depth"), lax.axis_size("plane")
    nz, nh, width = volume.shape
    chan = kernel_in.shape[1]
    sem = pltpu.SemaphoreType.DMA
    sel, selp, sely = selectors()
    lanes = 8 * 512 // plane
    per = 512 // lanes
    bins = ray_bins.reshape(32, 128)
    chosen = jnp.take(measured, angle_ids, axis=1)
    chosen = chosen.reshape(4, 8, 2, per, lanes).transpose(1, 3, 2, 0, 4)
    chosen = jnp.pad(chosen, ((0, 0), (0, 0), (0, 0), (0, 4), (0, 0))).reshape(plane, 16, lanes)

    s, r, slope1, slope2, a2, proj = call(
        functools.partial(forward_kernel, depth, plane, lanes),
        [((576, 128), BF), ((10, 960, 128), BF), ((6, 192, 128), F32), ((8, 256, 128), F32),
         ((6, 192, 128), BF), ((plane, 16, lanes), F32)],
        [pltpu.VMEM((9, 16, 128), BF), pltpu.VMEM((10 * chan, 144), BF),
         pltpu.VMEM((3 * chan, 9 * chan), BF), pltpu.VMEM((72, 6 * chan), BF), sem((9,)), sem((9,))],
        [volume.reshape(16, 128), sel, kernel_in, kernel_mid, kernel_out, selp,
         cotangent.reshape(16, 128), bins], 0)
    cot_rows = jnp.pad(cotangent.reshape(4, 512), ((0, 12), (0, 0)))
    gd, grad_slots, t4, w2b, t5 = call(
        functools.partial(rays_kernel, depth, plane, lanes),
        [((16, 512), F32), ((9, 16, 128), BF), ((8 * chan, 144), BF),
         ((3 * chan, 9 * chan), BF), ((72, 6 * chan), BF)],
        [pltpu.VMEM((8192, 512), BF), pltpu.VMEM((plane, 16, lanes), F32),
         pltpu.VMEM((16, lanes), BF), pltpu.VMEM((plane, 16, lanes), BF),
         pltpu.VMEM((16, 128), BF), pltpu.VMEM((9, 16, 128), BF),
         sem((plane,)), sem((plane,)), sem((plane,)), sem((plane,)), sem((9,)), sem((9,))],
        [proj, chosen, bins, cot_rows, sely, kernel_in, kernel_mid, kernel_out], 1)
    chunk = 16 * plane
    rows = -(-384 // chunk) * chunk
    each = rows // plane
    scale = float(nz * depth * nh * plane * width) ** -0.5
    adj, first, mid, third = call(
        functools.partial(backward_kernel, depth, plane, scale),
        [((4, 8, 128), F32), ((27, chan), F32), ((27, chan, chan), F32), ((27, chan), F32)],
        [pltpu.VMEM((rows, 128), F32),
         pltpu.VMEM((576, 128), BF), pltpu.VMEM((8, 768, 128), BF), pltpu.VMEM((6, 192, 128), BF),
         pltpu.VMEM((plane, each, 128), F32), pltpu.VMEM((each, 128), F32),
         pltpu.VMEM((depth, each, 128), F32), pltpu.VMEM((each, 128), BF),
         pltpu.VMEM((plane, each, 128), BF),
         sem((plane,)), sem((plane,)), sem((depth,)), sem((depth,)), sem((plane,)), sem((plane,))],
        [grad_slots, sel, t4, w2b, t5, s, r, slope1, slope2, a2], 2)
    grad_volume = gd[:4].reshape(4, 4, 128) + adj[:, 4:8, :]
    return (grad_volume, first, mid, third)


def solution(mesh):
    placed = (
        P("depth", "plane", None),
        P("depth", "plane", None),
        P(),
        P(),
        P(),
        P("depth", None, None),
        P(),
        P(None, "plane", None),
    )
    return jax.shard_map(
        per_device,
        mesh=mesh,
        in_specs=placed,
        out_specs=(P("depth", "plane", None), P(), P(), P()),
        check_vma=False,
    )
```

```python
import functools

import numpy as np
import jax
import jax.numpy as jnp
from jax import lax
from jax.experimental import pallas as pl
from jax.experimental.pallas import tpu as pltpu
from jax.sharding import PartitionSpec as P

MESH = pl.DeviceIdType.MESH
BF = jnp.bfloat16
F32 = jnp.float32
DELTA = 6.0
VMEM_LIMIT = 56 * 1024 * 1024
NT = (((1,), (1,)), ((), ()))


def mm(a, b):
    return jnp.dot(a, b, preferred_element_type=F32)


def mm_nt(a, b):
    return lax.dot_general(a, b, NT, preferred_element_type=F32)


def shift(x, j):
    if j == 1:
        return x
    width = x.shape[-1]
    lane = lax.broadcasted_iota(jnp.int32, x.shape, x.ndim - 1)
    if j == 0:
        return jnp.where(lane == 0, 0.0, pltpu.roll(x, 1, x.ndim - 1))
    return jnp.where(lane == width - 1, 0.0, pltpu.roll(x, width - 1, x.ndim - 1))


def sig(v):
    return 1.0 / (1.0 + jnp.exp(-v))


def halo_targets(depth, plane):
    d, p = lax.axis_index("depth"), lax.axis_index("plane")
    out = []
    for dz in (-1, 0, 1):
        for dy in (-1, 0, 1):
            if dz == 0 and dy == 0:
                continue
            there = (d + dz >= 0) & (d + dz < depth) & (p + dy >= 0) & (p + dy < plane)
            out.append((dz, dy, there, (d + dz, p + dy)))
    return out


def halo_copy(dz, dy, who, mine, slots, send, recv):
    slot = (1 - dz) * 3 + (1 - dy)
    return pltpu.make_async_remote_copy(
        src_ref=mine, dst_ref=slots.at[slot], send_sem=send.at[slot], recv_sem=recv.at[slot],
        device_id=who, device_id_type=MESH)


def halo_start(targets, mine, slots, send, recv):
    for dz, dy, there, who in targets:
        @pl.when(there)
        def _(dz=dz, dy=dy, who=who):
            halo_copy(dz, dy, who, mine, slots, send, recv).start()


def halo_wait(targets, mine, slots, send, recv):
    for dz, dy, there, who in targets:
        @pl.when(there)
        def _(dz=dz, dy=dy, who=who):
            halo_copy(dz, dy, who, mine, slots, send, recv).wait_send()
            halo_copy(-dz, -dy, who, mine, slots, send, recv).wait_recv()


def iota(shape, dim):
    return lax.broadcasted_iota(jnp.int32, shape, dim)


def ones_where(mask):
    return jnp.where(mask, 1.0, 0.0).astype(BF)


def tall(k, rows, off, flip):
    chan = k.shape[1]
    pick = ones_where(lax.rem(iota((rows * chan, chan), 0), chan) == iota((rows * chan, chan), 1))
    wide = mm_nt(pick, k).astype(BF)
    shape = (rows * chan, 144)
    y_in = lax.rem(iota(shape, 1), 16)
    y = iota(shape, 0) // chan
    col = iota((27, 144), 1)
    total = jnp.zeros(shape, F32)
    for jy in range(3):
        src = (col // 48) * 9 + jy * 3 + lax.rem(col // 16, 3)
        if flip:
            src = 26 - src
        part = mm(wide, ones_where(iota((27, 144), 0) == src))
        total = total + jnp.where(y_in == y + (off + jy - 1), part, 0.0)
    return total.astype(BF)


def flat(k, flip):
    chan = k.shape[1]
    shape = (72, 6 * chan)
    y = lax.rem(iota(shape, 0), 8)
    y_in = iota(shape, 1) // chan
    spread = ones_where(lax.rem(iota((chan, 6 * chan), 1), chan) == iota((chan, 6 * chan), 0))
    row = iota((72, 27), 0)
    total = jnp.zeros(shape, F32)
    for jy in range(3):
        src = lax.rem(row // 8, 3) * 9 + jy * 3 + row // 24
        if flip:
            src = 26 - src
        part = mm(mm(ones_where(iota((72, 27), 1) == src), k).astype(BF), spread)
        total = total + jnp.where((y >= 4) & (y_in == y - 4 + jy), part, 0.0)
    return total.astype(BF)


def square(k):
    chan = k.shape[1]
    total = jnp.zeros((3 * chan, 9 * chan), F32)
    for q in range(9):
        rows = jnp.concatenate([k[j * 9 + q] for j in range(3)], axis=0)
        place = ones_where(iota((chan, 9 * chan), 1) == iota((chan, 9 * chan), 0) + q * chan)
        total = total + mm(rows, place)
    return total.astype(BF)


def square_back(k):
    chan = k.shape[1]
    eye = ones_where(iota((chan, chan), 0) == iota((chan, chan), 1))
    return jnp.concatenate(
        [mm_nt(eye, jnp.concatenate([k[26 - j * 9 - q] for q in range(9)], axis=0))
         for j in range(3)], axis=0).astype(BF)


def fill_shifts(sel, slots, dst):
    flat = slots[...].reshape(9 * 16, 128)
    wide = mm(sel[...], flat)
    for z in range(12):
        rows = wide[z * 16:(z + 1) * 16]
        for j in range(3):
            dst[z * 48 + j * 16:z * 48 + (j + 1) * 16, :] = shift(rows, j).astype(BF)
    return wide


def keep_rows(shape, z, margin, depth, plane):
    d, p = lax.axis_index("depth"), lax.axis_index("plane")
    gz = d * 4 + z - margin
    row = lax.broadcasted_iota(jnp.int32, shape, 0)
    low = (margin - p * 4) * 32
    high = (plane * 4 + margin - p * 4) * 32
    high = jnp.where((gz >= 0) & (gz < depth * 4), high, -1)
    return (row >= low) & (row < high)


def build_onehot(bins, a, c, size):
    parts = []
    for y in range(4):
        row = bins[pl.ds(a * 4 + y, 1), :]
        at = lax.broadcasted_iota(jnp.int32, (size, 128), 0) + c * size
        parts.append(jnp.where(at == row, 1.0, 0.0).astype(BF))
    return jnp.concatenate(parts, axis=1)


def forward_kernel(depth, plane, lanes, block, sel, k1, k2, k3, selp, cot, bins,
                   s_out, r_out, slope1, slope2, a2, proj,
                   slots, t1, w2, t3, onehot, send, recv):
    targets = halo_targets(depth, plane)
    slots[...] = jnp.zeros_like(slots)
    bar = pltpu.get_barrier_semaphore()
    count = jnp.int32(0)
    for _, _, there, who in targets:
        @pl.when(there)
        def _(who=who):
            pl.semaphore_signal(bar, inc=1, device_id=who, device_id_type=MESH)
        count = count + there.astype(jnp.int32)
    pl.semaphore_wait(bar, count)
    halo_start(targets, block, slots, send, recv)
    t1[...] = tall(k1[...], 10, 1, False)
    w2[...] = square(k2)
    t3[...] = flat(k3[...], False)

    def fill(k, carry):
        onehot[pl.ds(pl.multiple_of(k * 256, 256), 256), :] = build_onehot(
            bins, k // 4, lax.rem(k, 4), 256)
        return carry

    lax.fori_loop(0, 32, fill, 0)
    halo_wait(targets, block, slots, send, recv)
    slots[4] = block[...]
    wide = fill_shifts(sel, slots, s_out)
    for z in range(10):
        pre = mm(t1[...], s_out[z * 48:z * 48 + 144, :])
        sg = sig(pre)
        keep = keep_rows(pre.shape, z, 3, depth, plane)
        act = jnp.where(keep, pre * sg, 0.0)
        for j in range(3):
            moved = shift(act, j).astype(BF)
            for y in range(10):
                r_out[z, y * 96 + j * 32:y * 96 + j * 32 + 32, :] = moved[y * 32:y * 32 + 32]
        if 2 <= z < 8:
            slope = jnp.where(keep, sg * (1.0 + pre * (1.0 - sg)), 0.0)
            slope1[z - 2] = slope[64:256]
    for y in range(0, 8, 2):
        res = []
        for z in range(10):
            rhs = jnp.concatenate(
                [r_out[z, y * 96:y * 96 + 288, :], r_out[z, y * 96 + 96:y * 96 + 384, :]], axis=1)
            res.append(mm(w2[...], rhs))
        for z in range(8):
            pre2 = res[z][0:32] + res[z + 1][32:64] + res[z + 2][64:96]
            for q in range(2):
                yy = y + q
                pre = pre2[:, q * 128:q * 128 + 128]
                sg = sig(pre)
                keep = keep_rows((256, 128), z, 2, depth, plane)[yy * 32:yy * 32 + 32]
                slope2[z, yy * 32:yy * 32 + 32, :] = jnp.where(
                    keep, sg * (1.0 + pre * (1.0 - sg)), 0.0)
                if 1 <= z < 7 and 1 <= yy < 7:
                    a2[z - 1, (yy - 1) * 32:yy * 32, :] = jnp.where(keep, pre * sg, 0.0).astype(BF)
    den = []
    res = [mm(t3[...], a2[z]) for z in range(6)]
    for z in range(4):
        total = wide[(z + 4) * 16:(z + 4) * 16 + 8]
        for j in range(3):
            part = res[z][j * 24:j * 24 + 8] + res[z + 1][j * 24 + 8:j * 24 + 16] \
                + res[z + 2][j * 24 + 16:j * 24 + 24]
            total = total - shift(part, j)
        den.append(total)
    both = jnp.concatenate(den + [cot[...]], axis=0)
    high = both.astype(BF)
    rest = (both - high.astype(F32)).astype(BF)
    stacked = mm(selp[...], jnp.concatenate([high, rest], axis=0)).astype(BF)
    lhs = jnp.concatenate([stacked[y * 16:y * 16 + 16] for y in range(4)], axis=1)
    per = 512 // lanes

    def view(a, carry):
        halves = []
        for half in range(2):
            row = []
            for c in range(2):
                at = pl.multiple_of(a * 1024 + (half * 2 + c) * 256, 256)
                got = mm_nt(lhs, onehot[pl.ds(at, 256), :])
                row.append(got[0:8] + got[8:16])
            halves.append(jnp.concatenate(row, axis=1))
        full = jnp.concatenate(halves, axis=0)
        for q in range(per):
            proj[a * per + q] = full[:, q * lanes:(q + 1) * lanes]
        return carry

    lax.fori_loop(0, 8, view, 0)


def rays_kernel(depth, plane, lanes, proj, chosen, bins, cot, sely, k1, k2, k3,
                gd_out, out, t4, w2, t5,
                onehot, got, mine, ag, block, slots, send1, recv1, send2, recv2, send3, recv3):
    d, p = lax.axis_index("depth"), lax.axis_index("plane")
    targets = halo_targets(depth, plane)
    slots[...] = jnp.zeros_like(slots)
    bar = pltpu.get_barrier_semaphore()
    count = jnp.int32(plane - 1)
    for i in range(1, plane):
        pl.semaphore_signal(bar, inc=1, device_id=(d, lax.rem(p + i, plane)), device_id_type=MESH)
    for dz, _, there, who in targets:
        if dz != 0:
            @pl.when(there)
            def _(who=who):
                pl.semaphore_signal(bar, inc=1, device_id=who, device_id_type=MESH)
            count = count + there.astype(jnp.int32)
    pl.semaphore_wait(bar, count)

    def first(i):
        to = lax.rem(p + i, plane)
        return pltpu.make_async_remote_copy(
            src_ref=proj.at[to], dst_ref=got.at[i], send_sem=send1.at[i], recv_sem=recv1.at[i],
            device_id=(d, to), device_id_type=MESH)

    def second(i):
        to = lax.rem(p + i, plane)
        return pltpu.make_async_remote_copy(
            src_ref=mine, dst_ref=ag.at[p], send_sem=send2.at[i], recv_sem=recv2.at[i],
            device_id=(d, to), device_id_type=MESH)

    for i in range(1, plane):
        first(i).start()

    def fill(k, carry):
        a = k // 4
        c = lax.rem(k, 4)
        onehot[pl.ds(pl.multiple_of(k * 256, 256), 256), :] = build_onehot(bins, a, c, 256)
        return carry

    lax.fori_loop(0, 32, fill, 0)
    t4[...] = tall(k3[...], 8, 2, True)
    w2[...] = square_back(k2)
    t5[...] = flat(k1[...], True)
    total = proj[p]
    for i in range(1, plane):
        first(i).wait_recv()
        total = total + got[i]
    ratio = (total - chosen[p]) / DELTA
    inner = 1.0 + ratio * ratio
    weighted = pltpu.roll(total, 12, 0) / (inner * jnp.sqrt(inner))
    lead = weighted.astype(BF).astype(F32)
    row = lax.rem(lax.broadcasted_iota(jnp.int32, weighted.shape, 0), 8)
    mine[...] = jnp.where(row < 4, lead, pltpu.roll(weighted - lead, 4, 0)).astype(BF)
    for i in range(1, plane):
        second(i).start()
    for i in range(1, plane):
        second(i).wait_recv()
        first(i).wait_send()
    for i in range(1, plane):
        second(i).wait_send()
    ag[p] = mine[...]
    per = 512 // lanes
    low = jnp.zeros((16, 512), F32)
    up = jnp.zeros((16, 512), F32)
    for a in range(8):
        lhs = jnp.concatenate([ag[a * per + q] for q in range(per)], axis=1)
        low = low + mm(lhs, onehot[a * 1024:a * 1024 + 512, :])
        up = up + mm(lhs, onehot[a * 1024 + 512:a * 1024 + 1024, :])
    up = pltpu.roll(up, 8, 0)
    back = low + up
    back = back + pltpu.roll(back, 12, 0)
    row = lax.broadcasted_iota(jnp.int32, (16, 512), 0)
    cot16 = jnp.concatenate([cot[...], jnp.zeros((12, 512), F32)], axis=0)
    gd = jnp.where(row < 4, cot16 - back * (0.25 / 8), 0.0)
    gd_out[...] = gd[0:4]
    neg = (-gd).astype(BF)
    total = jnp.zeros((16, 128), F32)
    for y in range(4):
        total = total + mm(sely[y], neg[:, y * 128:y * 128 + 128])
    block[...] = total.astype(BF)
    halo_start(targets, block, slots, send3, recv3)
    halo_wait(targets, block, slots, send3, recv3)
    out[...] = slots[...]
    out[4] = block[...]


def backward_kernel(depth, plane, slots, sel, t4, w2, t5, s, r, slope1, slope2, a2,
                    adj, out1, out2, out3, terms, sg, rm, gl,
                    got, part, other, mine, ag, s1, r1, s2, r2, s3, r3):
    d, p = lax.axis_index("depth"), lax.axis_index("plane")
    bar = pltpu.get_barrier_semaphore()
    for i in range(1, plane):
        pl.semaphore_signal(bar, inc=1, device_id=(d, lax.rem(p + i, plane)), device_id_type=MESH)
    for i in range(1, depth):
        pl.semaphore_signal(bar, inc=1, device_id=(lax.rem(d + i, depth), p), device_id_type=MESH)
    fill_shifts(sel, slots, sg)
    for z in range(8):
        grad = mm(t4[...], sg[(z + 1) * 48:(z + 1) * 48 + 144, :]) * slope2[z]
        for j in range(3):
            moved = shift(grad, j).astype(BF)
            for y in range(8):
                rm[z, y * 96 + j * 32:y * 96 + j * 32 + 32, :] = moved[y * 32:y * 32 + 32]
    for y in range(0, 6, 2):
        res = []
        for z in range(8):
            rhs = jnp.concatenate(
                [rm[z, y * 96:y * 96 + 288, :], rm[z, y * 96 + 96:y * 96 + 384, :]], axis=1)
            res.append(mm(w2[...], rhs))
        for z in range(6):
            grad = res[z][0:32] + res[z + 1][32:64] + res[z + 2][64:96]
            for q in range(2):
                yy = y + q
                at = slice(yy * 32, yy * 32 + 32)
                gl[z, at, :] = (grad[:, q * 128:q * 128 + 128] * slope1[z, at, :]).astype(BF)
    mid = jnp.zeros((288, 96), F32)
    none = jnp.zeros((32, 512), BF)
    own = [
        jnp.concatenate(
            [rm[z + 2, (y + 2) * 96 + 32:(y + 2) * 96 + 64, :] for y in range(4)], axis=1)
        for z in range(4)
    ]
    for t in range(6):
        lhs = jnp.concatenate(
            [r[t + 2, (y + 2) * 96:(y + 2) * 96 + 288, :] for y in range(4)], axis=1)
        rhs = jnp.concatenate(
            [own[t - j] if 0 <= t - j < 4 else none for j in range(3)], axis=0)
        mid = mid + mm_nt(lhs, rhs)
    terms[...] = jnp.zeros_like(terms)
    terms[0:288, 0:96] = mid
    first = jnp.zeros((144, 128), F32)
    for z in range(4):
        first = first + mm_nt(s[(z + 3) * 48:(z + 3) * 48 + 144, :], gl[z + 1, 32:160, :])
    third = jnp.zeros((144, 192), F32)
    blank = jnp.zeros((48, 128), BF)
    for t in range(6):
        lhs = jnp.concatenate(
            [sg[(4 + t - j) * 48:(5 + t - j) * 48, :] if 0 <= t - j < 4 else blank
             for j in range(3)], axis=0)
        third = third + mm_nt(lhs, a2[t])
    third = jnp.concatenate([third, jnp.zeros((144, 64), F32)], axis=1)
    row = lax.rem(lax.broadcasted_iota(jnp.int32, (144, 128), 0), 16)
    group = lax.broadcasted_iota(jnp.int32, (144, 128), 1) // 32
    for jy in range(3):
        pick = jnp.where(row == group + (3 + jy), first, 0.0).reshape(9, 16, 128).sum(axis=1)
        terms[288 + jy * 16:288 + jy * 16 + 16, :] = jnp.concatenate(
            [pick, jnp.zeros((7, 128), F32)], axis=0)
        own_row = (row >= 4) & (row < 8)
        pick = jnp.where(own_row & (row - 4 + jy == group), third[:, 0:128], 0.0) \
            + jnp.where(own_row & (row - 4 + jy == group + 4), third[:, 128:256], 0.0)
        pick = pick.reshape(9, 16, 128).sum(axis=1)
        terms[336 + jy * 16:336 + jy * 16 + 16, :] = jnp.concatenate(
            [pick, jnp.zeros((7, 128), F32)], axis=0)
    pl.semaphore_wait(bar, plane + depth - 2)
    each = terms.shape[0] // plane

    def rows_of(q):
        return terms.at[pl.ds(pl.multiple_of(q * each, each), each)]

    def first(i):
        to = lax.rem(p + i, plane)
        return pltpu.make_async_remote_copy(
            src_ref=rows_of(to), dst_ref=got.at[i], send_sem=s1.at[i], recv_sem=r1.at[i],
            device_id=(d, to), device_id_type=MESH)

    def second(i):
        return pltpu.make_async_remote_copy(
            src_ref=part, dst_ref=other.at[i], send_sem=s2.at[i], recv_sem=r2.at[i],
            device_id=(lax.rem(d + i, depth), p), device_id_type=MESH)

    def third(i):
        return pltpu.make_async_remote_copy(
            src_ref=mine, dst_ref=ag.at[p], send_sem=s3.at[i], recv_sem=r3.at[i],
            device_id=(d, lax.rem(p + i, plane)), device_id_type=MESH)

    for i in range(1, plane):
        first(i).start()
    res = [mm(t5[...], gl[z]) for z in range(6)]
    for z in range(4):
        total = jnp.zeros((8, 128), F32)
        for j in range(3):
            piece = res[z][j * 24:j * 24 + 8] + res[z + 1][j * 24 + 8:j * 24 + 16] \
                + res[z + 2][j * 24 + 16:j * 24 + 24]
            total = total + shift(piece, j)
        adj[z] = total
    total = rows_of(p)[...]
    for i in range(1, plane):
        first(i).wait_recv()
        total = total + got[i]
    part[...] = total
    for i in range(1, depth):
        second(i).start()
    for i in range(1, depth):
        second(i).wait_recv()
    other[0] = total
    total = jnp.zeros_like(total)
    for k in range(depth):
        total = total + other[lax.rem(d - k + depth, depth)]
    mine[...] = total.astype(BF)
    for i in range(1, plane):
        third(i).start()
    for i in range(1, plane):
        third(i).wait_recv()
        first(i).wait_send()
        third(i).wait_send()
    for i in range(1, depth):
        second(i).wait_send()
    ag[p] = mine[...]
    summed = ag[...].reshape(plane * each, 128)
    chan = out2.shape[1]
    for j in range(3):
        pick = ones_where(iota((chan, 128), 1) == iota((chan, 128), 0) + j * chan)
        for q in range(9):
            out2[j * 9 + q] = mm_nt(pick, summed[q * chan:(q + 1) * chan])
    fold = ones_where(lax.rem(iota((128, chan), 0), chan) == iota((128, chan), 1))
    k = iota((32, 48), 0)
    for at, flip, out in ((288, False, out1), (336, True, out3)):
        jx = lax.rem(k, 3)
        jx = 2 - jx if flip else jx
        order = ones_where(iota((32, 48), 1) == lax.rem(k // 3, 3) * 16 + (k // 9) * 3 + jx)
        moved = mm(order, summed[at:at + 48]).astype(BF)
        out[...] = mm(moved, fold)[0:27]


def selectors():
    sel = np.zeros((192, 144), np.float32)
    for z in range(12):
        for y in range(12):
            sel[z * 16 + y, ((z // 4) * 3 + y // 4) * 16 + (z % 4) * 4 + y % 4] = 1.0
    selp = np.zeros((64, 96), np.float32)
    for y in range(4):
        for z in range(4):
            for k in range(2):
                selp[y * 16 + k * 8 + z, k * 48 + z * 8 + 4 + y] = 1.0
                selp[y * 16 + k * 8 + 4 + z, k * 48 + 32 + z * 4 + y] = 1.0
    sely = np.zeros((4, 16, 16), np.float32)
    for y in range(4):
        for z in range(4):
            sely[y, z * 4 + y, z] = 1.0
    return [jnp.asarray(x, BF) for x in (sel, selp, sely)]


def call(body, outs, scratch, args, cid=None):
    vm = pl.BlockSpec(memory_space=pltpu.VMEM)
    extra = {} if cid is None else dict(collective_id=cid, has_side_effects=True)
    return pl.pallas_call(
        body,
        out_shape=[jax.ShapeDtypeStruct(s, t) for s, t in outs],
        in_specs=[vm] * len(args),
        out_specs=[vm] * len(outs),
        scratch_shapes=scratch,
        compiler_params=pltpu.CompilerParams(vmem_limit_bytes=VMEM_LIMIT, **extra),
    )(*args)


def per_device(volume, cotangent, kernel_in, kernel_mid, kernel_out, measured, angle_ids, ray_bins):
    depth, plane = lax.axis_size("depth"), lax.axis_size("plane")
    nz, nh, width = volume.shape
    chan = kernel_in.shape[1]
    sem = pltpu.SemaphoreType.DMA
    sel, selp, sely = selectors()
    lanes = 8 * 512 // plane
    per = 512 // lanes
    bins = ray_bins.reshape(32, 128)
    chosen = jnp.take(measured, angle_ids, axis=1)
    chosen = chosen.reshape(4, 8, 2, per, lanes).transpose(1, 3, 2, 0, 4)
    chosen = jnp.pad(chosen, ((0, 0), (0, 0), (0, 0), (0, 4), (0, 0))).reshape(plane, 16, lanes)

    s, r, slope1, slope2, a2, proj = call(
        functools.partial(forward_kernel, depth, plane, lanes),
        [((576, 128), BF), ((10, 960, 128), BF), ((6, 192, 128), F32), ((8, 256, 128), F32),
         ((6, 192, 128), BF), ((plane, 16, lanes), F32)],
        [pltpu.VMEM((9, 16, 128), BF), pltpu.VMEM((10 * chan, 144), BF),
         pltpu.VMEM((3 * chan, 9 * chan), BF), pltpu.VMEM((72, 6 * chan), BF),
         pltpu.VMEM((8192, 512), BF), sem((9,)), sem((9,))],
        [volume.reshape(16, 128), sel, kernel_in, kernel_mid, kernel_out, selp,
         cotangent.reshape(16, 128), bins], 0)
    cot_rows = cotangent.reshape(4, 512)
    gd, grad_slots, t4, w2b, t5 = call(
        functools.partial(rays_kernel, depth, plane, lanes),
        [((4, 512), F32), ((9, 16, 128), BF), ((8 * chan, 144), BF),
         ((3 * chan, 9 * chan), BF), ((72, 6 * chan), BF)],
        [pltpu.VMEM((8192, 512), BF), pltpu.VMEM((plane, 16, lanes), F32),
         pltpu.VMEM((16, lanes), BF), pltpu.VMEM((plane, 16, lanes), BF),
         pltpu.VMEM((16, 128), BF), pltpu.VMEM((9, 16, 128), BF),
         sem((plane,)), sem((plane,)), sem((plane,)), sem((plane,)), sem((9,)), sem((9,))],
        [proj, chosen, bins, cot_rows, sely, kernel_in, kernel_mid, kernel_out], 1)
    chunk = 16 * plane
    rows = -(-384 // chunk) * chunk
    each = rows // plane
    scale = float(nz * depth * nh * plane * width) ** -0.5
    adj, first, mid, third = call(
        functools.partial(backward_kernel, depth, plane),
        [((4, 8, 128), F32), ((27, chan), F32), ((27, chan, chan), F32), ((27, chan), F32)],
        [pltpu.VMEM((rows, 128), F32),
         pltpu.VMEM((576, 128), BF), pltpu.VMEM((8, 768, 128), BF), pltpu.VMEM((6, 192, 128), BF),
         pltpu.VMEM((plane, each, 128), F32), pltpu.VMEM((each, 128), F32),
         pltpu.VMEM((depth, each, 128), F32), pltpu.VMEM((each, 128), BF),
         pltpu.VMEM((plane, each, 128), BF),
         sem((plane,)), sem((plane,)), sem((depth,)), sem((depth,)), sem((plane,)), sem((plane,))],
        [grad_slots, sel, t4, w2b, t5, s, r, slope1, slope2, a2], 2)
    grad_volume = gd.reshape(4, 4, 128) + adj[:, 4:8, :]
    return (grad_volume, first * scale, mid * scale, third * scale)


def solution(mesh):
    placed = (
        P("depth", "plane", None),
        P("depth", "plane", None),
        P(),
        P(),
        P(),
        P("depth", None, None),
        P(),
        P(None, "plane", None),
    )
    return jax.shard_map(
        per_device,
        mesh=mesh,
        in_specs=placed,
        out_specs=(P("depth", "plane", None), P(), P(), P()),
        check_vma=False,
    )
```
